512 devices in a mesh: rollout: 32 (over z, x), mp: 16 (over y, core).
Axes of the slice: x: 4, y: 8, z: 8, core: 2. Of those that a mesh axis runs over, the one named last changes fastest.
Arguments:
- queries: bfloat16 [128, 256, 8192], P('rollout', None, 'mp'), may hold values from -6 to 6
- keys: bfloat16 [128, 256, 8192], P('rollout', None, 'mp'), may hold values from -0.5 to 0.5
- values_in: bfloat16 [128, 256, 8192], P('rollout', None, 'mp'), may hold values from -64 to 64
- state_in: bfloat16 [128, 64, 16384], P('rollout', 'mp'), may hold values from -6 to 6
- decay_rate: float32 [64], P('mp'), may hold values from 0.0005 to 0.05
- norm_gain: float32 [8192], P('mp'), may hold values from 0.25 to 1.75
- turn_len: int32 [128], P('rollout'), may hold values from 1 to 256, as said below
- relocation: int32 [128], replicated, may hold values from 0 to 127, as said below
Outputs:
- layer_out: bfloat16 [128, 256, 8192], P('rollout', None, 'mp')
- state_out: bfloat16 [128, 64, 16384], P('rollout', 'mp')
The draws below stay inside these ranges and needn't reach their ends.
Inputs may be any that keep to these rules, and one draw needn't show every extreme that they name: `relocation`: A permutation: entry g is the new position of the conversation at old position g. A conversation keeps its place within its block of 4 positions (new minus old position is a multiple of 4), and the 4 conversations of one block go to 4 different blocks. `turn_len`: the longest turn has exactly 256 tokens.
All inputs are finite; a program needn't handle non-finite values.
Results may differ from the reference program's by a relative error of at most 0.0049.
Values may be sent and summed in bfloat16 or wider, within the bound.
A program may use at most 64 MiB of HBM per device.

```python
import math
import jax
import jax.numpy as jnp
from jax import lax

HD = 128
TURN = 256
CONV_DEV = 4
HEADS = 64
CONVS = 128


def draw_values_in(key, part):
    key = jax.random.fold_in(key, 2)
    first = jax.random.fold_in(key, 0)
    column = jnp.arange(HEADS * HD) // HD
    frac = column.astype(jnp.float32) / max(HEADS - 1, 1)
    base = jnp.clip(jax.random.normal(first, (CONVS, TURN, HEADS * HD), jnp.float32), -6.0, 6.0)
    result = base * 3.0 ** frac
    return result.astype(jnp.bfloat16)


def draw_turn_len(key, part):
    key = jax.random.fold_in(key, 3)
    first, second = jax.random.split(key)
    lengths = jax.random.randint(first, (CONVS,), 1, TURN + 1)
    where_full = jax.random.randint(second, (), 0, CONVS)
    return lengths.at[where_full].set(TURN).astype(jnp.int32)


def draw_relocation(key, part):
    key = jax.random.fold_in(key, 4)
    first, second, third = jax.random.split(key, 3)
    blocks = CONVS // CONV_DEV
    sigma = jax.random.permutation(first, blocks)
    rho = jax.random.permutation(second, blocks)
    shifts = jax.random.permutation(third, blocks)[:CONV_DEV]
    source_block = jnp.arange(blocks)[:, None]
    within_block = jnp.arange(CONV_DEV)[None, :]
    target = sigma[(rho[source_block] + shifts[within_block]) % blocks]
    return (target * CONV_DEV + within_block).reshape(-1).astype(jnp.int32)


def block_levels(own_key, shape, cuts, smallest, high):
    def one(axis_at, blocks):
        steps = jax.random.uniform(jax.random.fold_in(jax.random.fold_in(own_key, 6), axis_at), (blocks,), jnp.float32, smallest / len(cuts), high / len(cuts))
        return jnp.repeat(jnp.exp(steps), shape[axis_at] // blocks).reshape((-1,) + (1,) * (len(shape) - axis_at - 1))

    gain = one(*cuts[0])
    for cut in cuts[1:]:
        gain = gain * one(*cut)
    return gain


def normal_values(own_key, extent, spread, reach, pieces=(), held_as=jnp.bfloat16):
    loudness = block_levels(own_key, extent, pieces, -0.22, 0.18) if pieces else 1.0
    drawn = jax.random.normal(own_key, extent, jnp.float32) * spread * loudness
    return jnp.minimum(jnp.maximum(drawn, -reach), reach).astype(held_as)


def setup_inputs(seed: int = 0) -> dict:
    splits = jax.random.split(jax.random.key(seed), 9)
    queries = normal_values(splits[0], (CONVS, TURN, HEADS * HD), 1.0, 6.0, ((0, 32), (2, 16)))
    keys = normal_values(splits[1], (CONVS, TURN, HEADS * HD), HD ** -0.5, 0.5, ((0, 32), (2, 16)))
    values_in = draw_values_in(jax.random.fold_in(splits[8], 71), 0)
    state_in = normal_values(splits[3], (CONVS, HEADS, HD * HD), 1.0, 6.0, ((0, 32), (1, 16)))
    decay_rate = jnp.clip(jnp.exp(math.log(0.05) - 4.6051702 * jax.random.uniform(splits[4], (HEADS,), jnp.float32) ** block_levels(splits[4], (HEADS,), ((0, 16),), -0.2, 0.2)), 0.0005, 0.05)
    norm_gain = jnp.clip(1.0 + 0.15 * jax.random.normal(splits[5], (HEADS * HD,), jnp.float32), 0.25, 1.75)
    turn_len = draw_turn_len(jax.random.fold_in(splits[8], 71), 0)
    relocation = draw_relocation(jax.random.fold_in(splits[8], 71), 0)
    return {"queries": queries, "keys": keys, "values_in": values_in, "state_in": state_in, "decay_rate": decay_rate, "norm_gain": norm_gain, "turn_len": turn_len, "relocation": relocation}


epsilon = 1e-05

def reference(queries, keys, values_in, state_in, decay_rate, norm_gain, turn_len, relocation):
    carried = jnp.zeros_like(state_in).at[relocation].set(state_in)
    places = jnp.arange(TURN, dtype=jnp.float32)
    index_row = jnp.arange(TURN, dtype=jnp.int32)
    spacing = jnp.maximum(places[:, None] - places[None, :], 0.0)
    decay_grid = jnp.exp(-decay_rate[:, None, None] * spacing[None])
    causal = index_row[:, None] >= index_row[None, :]

    def one_conv(items):
        query_row, key_row, value_row, held, length = items
        q_heads = query_row.astype(jnp.float32).reshape(TURN, HEADS, HD)
        k_heads = key_row.astype(jnp.float32).reshape(TURN, HEADS, HD)
        v_heads = value_row.astype(jnp.float32).reshape(TURN, HEADS, HD)
        live_rows = index_row < length
        scores = jnp.einsum('thd,shd->hts', q_heads, k_heads)
        allowed = causal[None] & live_rows[None, :, None]
        weights = jnp.where(allowed, scores * decay_grid, 0.0)
        weights = lax.optimization_barrier(weights.astype(jnp.bfloat16)).astype(jnp.float32)
        within = jnp.einsum('hts,shd->thd', weights, v_heads)
        held_grid = held.astype(jnp.float32).reshape(HEADS, HD, HD)
        carried_term = jnp.einsum('thd,hde->the', q_heads, held_grid)
        carried_term = carried_term * jnp.exp(-decay_rate[None, :] * (places[:, None] + 1.0))[:, :, None]
        attended = jnp.where(live_rows[:, None, None], within + carried_term, 0.0)
        mean_sq = lax.optimization_barrier(jnp.mean(attended * attended, axis=(1, 2)))
        layer_row = (attended.reshape(TURN, HEADS * HD) * lax.rsqrt(mean_sq + epsilon)[:, None] * norm_gain).astype(jnp.bfloat16)
        len_float = length.astype(jnp.float32)
        remain = jnp.maximum(len_float - 1.0 - places, 0.0)
        kweight = jnp.exp(-decay_rate[None, :] * remain[:, None])
        decayed = jnp.where(live_rows[:, None, None], k_heads * kweight[:, :, None], 0.0)
        decayed = lax.optimization_barrier(decayed.astype(jnp.bfloat16)).astype(jnp.float32)
        update = jnp.einsum('shd,she->hde', decayed, v_heads)
        new_state = jnp.exp(-decay_rate * len_float)[:, None, None] * held_grid + update
        return (layer_row, new_state.reshape(HEADS, HD * HD).astype(jnp.bfloat16))
    layer_out, state_out = lax.map(one_conv, (queries, keys, values_in, carried, turn_len))
    return (layer_out, state_out)
```

```python
import functools

import jax
import jax.numpy as jnp
from jax import lax
from jax.experimental import pallas as pl
from jax.experimental.pallas import tpu as pltpu
from jax.sharding import PartitionSpec as P

EPS = 1e-05
MESH = pl.DeviceIdType.MESH
HD = 128
TURN = 256
CONV = 4
HEADS = 4
WIDTH = HEADS * HD
ROWS = HEADS * HD
CHUNKS = 2
PER = CONV // CHUNKS
NX = 4
HIGH = lax.Precision.HIGHEST


def turn_order(count):
    return sorted(range(count), key=lambda d: -min(d, count - d))


def kernel(
    nb, nm,
    decay_ref, len_ref, src_ref, gain_ref, q_hbm, k_hbm, v_hbm, state_hbm,
    out_hbm, state_out_hbm,
    q, k, v, att, upd, grid, qdec, outg, carr, wide, sums, out, sout,
    load_sem, a_send, a_recv, b_send, b_recv, m_send, m_recv, out_sem, *gath,
):
    me = lax.axis_index("rollout")
    m = lax.axis_index("mp")
    nx = min(NX, nb)
    nz = nb // nx
    z = me // nx
    x = lax.rem(me, nx)
    rows = ROWS // nb
    peers = []
    for dz in turn_order(nz):
        for dx in turn_order(nx):
            if dz or dx:
                peers.append(lax.rem(z + dz, nz) * nx + lax.rem(x + dx, nx))

    barrier = pltpu.get_barrier_semaphore()
    for t in peers:
        pl.semaphore_signal(barrier, inc=1, device_id=(t, m), device_id_type=MESH)
    for d in range(1, nm):
        pl.semaphore_signal(
            barrier, inc=1, device_id=(me, lax.rem(m + d, nm)), device_id_type=MESH
        )
    loads = [
        pltpu.make_async_copy(hbm, vmem, load_sem.at[n])
        for n, (hbm, vmem) in enumerate(((k_hbm, k), (v_hbm, v), (q_hbm, q)))
    ]
    for copy in loads:
        copy.start()
    pl.semaphore_wait(barrier, nb - 1 + nm - 1)

    def piece(t):
        return pl.ds(pl.multiple_of(t * rows, rows), rows)

    def spread(c, t):
        return state_hbm.at[pl.ds(c * PER, PER), piece(t), :], gath[c].at[me]

    def deliver(c, t):
        return outg.at[c, t], carr.at[pl.ds(c * PER, PER), piece(me), :]

    def send_all(c, which, send_sem, recv_sem):
        for t in peers:
            source, target = which(c, t)
            pltpu.make_async_remote_copy(
                src_ref=source, dst_ref=target, send_sem=send_sem.at[c],
                recv_sem=recv_sem.at[c], device_id=(t, m), device_id_type=MESH,
            ).start()
        source, target = which(c, me)
        pltpu.make_async_copy(source, target, recv_sem.at[c]).start()

    def wait_bytes(ref, sem):
        pltpu.make_async_copy(ref, ref, sem).wait()

    for c in range(CHUNKS):
        send_all(c, spread, a_send, a_recv)

    t_idx = lax.broadcasted_iota(jnp.int32, (TURN, TURN), 0)
    s_idx = lax.broadcasted_iota(jnp.int32, (TURN, TURN), 1)
    spacing = jnp.maximum(t_idx - s_idx, 0).astype(jnp.float32)
    causal = t_idx >= s_idx
    row_i = lax.broadcasted_iota(jnp.int32, (TURN, HD), 0)
    row_f = row_i.astype(jnp.float32)
    for h in range(HEADS):
        grid[h] = jnp.where(causal, jnp.exp(-decay_ref[h] * spacing), 0.0)
        qdec[h] = jnp.exp(-decay_ref[h] * (row_f + 1.0))
    for copy in loads:
        copy.wait()

    def local(j, _):
        length = len_ref[j]
        live = row_i < length
        remain = jnp.maximum(length.astype(jnp.float32) - 1.0 - row_f, 0.0)
        for h in range(HEADS):
            cols = slice(h * HD, (h + 1) * HD)
            qh, kh, vh = q[j, :, cols], k[j, :, cols], v[j, :, cols]
            scores = lax.dot_general(
                qh, kh, (((1,), (1,)), ((), ())), preferred_element_type=jnp.float32
            )
            weights = (scores * grid[h]).astype(jnp.bfloat16)
            att[j, :, cols] = jnp.dot(weights, vh, preferred_element_type=jnp.float32)
            kdec = jnp.where(
                live, kh.astype(jnp.float32) * jnp.exp(-decay_ref[h] * remain), 0.0
            ).astype(jnp.bfloat16)
            upd[j, h] = lax.dot_general(
                kdec, vh, (((0,), (0,)), ((), ())), preferred_element_type=jnp.float32
            )
        return 0

    lax.fori_loop(0, CONV, local, 0)

    for c in range(CHUNKS):
        wait_bytes(gath[c], a_recv.at[c])

        def pick(d, _):
            for jj in range(PER):
                outg[c, d, jj] = gath[c][src_ref[d * CONV + c * PER + jj], jj]
            return 0

        lax.fori_loop(0, nb, pick, 0)
        send_all(c, deliver, b_send, b_recv)

    for c in range(CHUNKS):
        wait_bytes(carr.at[pl.ds(c * PER, PER)], b_recv.at[c])

        def finish(jj, _):
            j = c * PER + jj
            length = len_ref[j]
            live = row_i < length
            wide[0] = carr[j].astype(jnp.float32)
            square = jnp.zeros((TURN, HD), jnp.float32)
            for h in range(HEADS):
                cols = slice(h * HD, (h + 1) * HD)
                held = wide[0, pl.ds(h, HD, stride=HEADS), :]
                term = jnp.dot(
                    q[j, :, cols], held.astype(jnp.bfloat16), preferred_element_type=jnp.float32
                )
                a = jnp.where(live, att[j, :, cols] + term * qdec[h], 0.0)
                att[j, :, cols] = a
                square = square + a * a
                keep = jnp.exp(
                    jnp.full((HD, HD), -decay_ref[h] * length.astype(jnp.float32), jnp.float32)
                )
                wide[1, pl.ds(h, HD, stride=HEADS), :] = keep * held + upd[j, h]
            sout[j] = wide[1].astype(jnp.bfloat16)
            row = lax.dot_general(
                jnp.ones((8, HD), jnp.float32), square, (((1,), (1,)), ((), ())),
                preferred_element_type=jnp.float32, precision=HIGH,
            )
            sums[c, m, pl.ds(jj, 1), :] = row[0:1]
            return 0

        for jj in range(PER):
            finish(jj, 0)
        for d in range(1, nm):
            pltpu.make_async_remote_copy(
                src_ref=sums.at[c, m], dst_ref=sums.at[c, m], send_sem=m_send.at[c, d],
                recv_sem=m_recv.at[c, d], device_id=(me, lax.rem(m + d, nm)),
                device_id_type=MESH,
            ).start()
        pltpu.make_async_copy(
            sout.at[pl.ds(c * PER, PER)], state_out_hbm.at[pl.ds(c * PER, PER)], out_sem.at[0, c]
        ).start()

    for c in range(CHUNKS):
        for d in range(1, nm):
            pltpu.make_async_remote_copy(
                src_ref=sums.at[c, m], dst_ref=sums.at[c, m], send_sem=m_send.at[c, d],
                recv_sem=m_recv.at[c, d], device_id=(me, lax.rem(m + d, nm)),
                device_id_type=MESH,
            ).wait()
        for jj in range(PER):
            j = c * PER + jj
            total = lax.dot_general(
                sums[c, :, jj, :], jnp.ones((nm, HD), jnp.float32), (((0,), (0,)), ((), ())),
                preferred_element_type=jnp.float32, precision=HIGH,
            )
            scale = lax.rsqrt(total / (nm * WIDTH) + EPS)
            for h in range(HEADS):
                cols = slice(h * HD, (h + 1) * HD)
                out[j, :, cols] = (att[j, :, cols] * scale * gain_ref[:, cols]).astype(jnp.bfloat16)
        pltpu.make_async_copy(
            out.at[pl.ds(c * PER, PER)], out_hbm.at[pl.ds(c * PER, PER)], out_sem.at[1, c]
        ).start()

    for c in range(CHUNKS):
        wait_bytes(gath[c].at[pl.ds(0, nb - 1)], a_send.at[c])
        wait_bytes(outg.at[c, pl.ds(0, nb - 1)], b_send.at[c])
        wait_bytes(sout.at[pl.ds(c * PER, PER)], out_sem.at[0, c])
        wait_bytes(out.at[pl.ds(c * PER, PER)], out_sem.at[1, c])


def per_device(nb, nm, queries, keys, values_in, state_in, decay_rate, norm_gain, turn_len, relocation):
    convs = relocation.shape[0]
    places = jnp.arange(convs, dtype=jnp.int32)
    src_block = jnp.sum(
        jnp.where(relocation[None, :] == places[:, None], places[None, :] // CONV, 0), axis=1
    ).astype(jnp.int32)
    state = state_in.reshape(CONV, HEADS, HD, HD).transpose(0, 2, 1, 3).reshape(CONV, ROWS, HD)
    rows = ROWS // nb
    bf16, f32 = jnp.bfloat16, jnp.float32
    smem = pl.BlockSpec(memory_space=pltpu.SMEM)
    hbm = pl.BlockSpec(memory_space=pl.ANY)
    layer_out, state_out = pl.pallas_call(
        functools.partial(kernel, nb, nm),
        out_shape=(
            jax.ShapeDtypeStruct((CONV, TURN, WIDTH), bf16),
            jax.ShapeDtypeStruct((CONV, ROWS, HD), bf16),
        ),
        in_specs=[smem, smem, smem, pl.BlockSpec(memory_space=pltpu.VMEM), hbm, hbm, hbm, hbm],
        out_specs=(hbm, hbm),
        scratch_shapes=[
            pltpu.VMEM((CONV, TURN, WIDTH), bf16),
            pltpu.VMEM((CONV, TURN, WIDTH), bf16),
            pltpu.VMEM((CONV, TURN, WIDTH), bf16),
            pltpu.VMEM((CONV, TURN, WIDTH), f32),
            pltpu.VMEM((CONV, HEADS, HD, HD), f32),
            pltpu.VMEM((HEADS, TURN, TURN), f32),
            pltpu.VMEM((HEADS, TURN, HD), f32),
            pltpu.VMEM((CHUNKS, nb, PER, rows, HD), bf16),
            pltpu.VMEM((CONV, ROWS, HD), bf16),
            pltpu.VMEM((2, ROWS, HD), f32),
            pltpu.VMEM((CHUNKS, nm, PER, TURN), f32),
            pltpu.VMEM((CONV, TURN, WIDTH), bf16),
            pltpu.VMEM((CONV, ROWS, HD), bf16),
            pltpu.SemaphoreType.DMA((3,)),
            pltpu.SemaphoreType.DMA((CHUNKS,)),
            pltpu.SemaphoreType.DMA((CHUNKS,)),
            pltpu.SemaphoreType.DMA((CHUNKS,)),
            pltpu.SemaphoreType.DMA((CHUNKS,)),
            pltpu.SemaphoreType.DMA((CHUNKS, nm)),
            pltpu.SemaphoreType.DMA((CHUNKS, nm)),
            pltpu.SemaphoreType.DMA((2, CHUNKS)),
        ] + [pltpu.VMEM((nb, PER, rows, HD), bf16)] * CHUNKS,
        compiler_params=pltpu.CompilerParams(
            collective_id=0, has_side_effects=True, vmem_limit_bytes=58 << 20
        ),
    )(
        decay_rate, turn_len, src_block, norm_gain.reshape(1, WIDTH),
        queries, keys, values_in, state,
    )
    state_out = state_out.reshape(CONV, HD, HEADS, HD).transpose(0, 2, 1, 3)
    return layer_out, state_out.reshape(CONV, HEADS, HD * HD)


def solution(mesh):
    nb, nm = mesh.shape["rollout"], mesh.shape["mp"]
    in_specs = (
        P("rollout", None, "mp"),
        P("rollout", None, "mp"),
        P("rollout", None, "mp"),
        P("rollout", "mp", None),
        P("mp"),
        P("mp"),
        P("rollout"),
        P(),
    )
    out_specs = (P("rollout", None, "mp"), P("rollout", "mp", None))
    return jax.shard_map(
        functools.partial(per_device, nb, nm),
        mesh=mesh, in_specs=in_specs, out_specs=out_specs, check_vma=False,
    )
```

```python
import functools

import jax
import jax.numpy as jnp
from jax import lax
from jax.experimental import pallas as pl
from jax.experimental.pallas import tpu as pltpu
from jax.sharding import PartitionSpec as P

EPS = 1e-05
MESH = pl.DeviceIdType.MESH
HD = 128
TURN = 256
CONV = 4
HEADS = 4
WIDTH = HEADS * HD
ROWS = HEADS * HD
CHUNKS = 2
ORDER = [(dz, dx) for dz in (4, 3, 5, 2, 6, 1, 7, 0) for dx in (2, 1, 3, 0) if dz or dx]
PER = CONV // CHUNKS
NX = 4
HIGH = lax.Precision.HIGHEST


def wait_bytes(ref, sem):
    pltpu.make_async_copy(ref, ref, sem).wait()


def kernel(
    nx, nz, nm,
    decay_hbm, len_hbm, reloc_hbm, gain_hbm, q_hbm, k_hbm, v_hbm, state_hbm,
    out, sout,
    decay_ref, len_ref, src_ref, src_row, reloc_ref, gain_ref,
    q, k, v, att, upd, grid, qdec, outg, carr, wide, sums,
    small_sem, load_sem, a_sem, b_sem, m_sem, *gath,
):
    nb = nz * nx
    me = lax.axis_index("rollout")
    m = lax.axis_index("mp")
    z = me // nx
    x = lax.rem(me, nx)
    rows = ROWS // nb

    def peer(dz, dx):
        return lax.rem(z + dz, nz) * nx + lax.rem(x + dx, nx)

    peers = [peer(dz, dx) for dz, dx in ORDER if dz < nz and dx < nx]
    barrier = pltpu.get_barrier_semaphore()
    for t in reversed(peers):
        pl.semaphore_signal(barrier, inc=1, device_id=(t, m), device_id_type=MESH)
    for d in range(1, nm):
        pl.semaphore_signal(barrier, inc=1, device_id=(me, lax.rem(m + d, nm)), device_id_type=MESH)

    def piece(t):
        return pl.ds(pl.multiple_of(t * rows, rows), rows)

    def convs(c):
        return pl.ds(c * PER, PER)

    loads = [
        pltpu.make_async_copy(source, target, small_sem.at[n])
        for n, (source, target) in enumerate((
            (reloc_hbm, reloc_ref), (decay_hbm, decay_ref), (len_hbm, len_ref), (gain_hbm, gain_ref),
        ))
    ] + [
        pltpu.make_async_copy(source, target, load_sem.at[n])
        for n, (source, target) in enumerate(((k_hbm, k), (v_hbm, v), (q_hbm, q)))
    ]
    for copy in loads:
        copy.start()
    pl.semaphore_wait(barrier, nb - 1 + nm - 1)

    for c in range(CHUNKS):
        for t in peers:
            pltpu.make_async_remote_copy(
                src_ref=state_hbm.at[convs(c), piece(t), :], dst_ref=gath[c].at[me],
                send_sem=a_sem.at[0, c], recv_sem=a_sem.at[1, c],
                device_id=(t, m), device_id_type=MESH,
            ).start()
        pltpu.make_async_copy(
            state_hbm.at[convs(c), piece(me), :], gath[c].at[me], a_sem.at[1, c]
        ).start()

    for copy in loads[:4]:
        copy.wait()
    places = src_row.shape[1]
    came = jnp.broadcast_to(reloc_ref[...], (places, places)).T
    old = lax.broadcasted_iota(jnp.int32, (places, places), 0) // CONV
    place = lax.broadcasted_iota(jnp.int32, (places, places), 1)
    src_row[...] = jnp.max(jnp.where(came == place, old, 0), axis=0, keepdims=True)
    to_scalars = pltpu.make_async_copy(src_row, src_ref, small_sem.at[4])
    to_scalars.start()

    t_idx = lax.broadcasted_iota(jnp.int32, (TURN, TURN), 0)
    s_idx = lax.broadcasted_iota(jnp.int32, (TURN, TURN), 1)
    spacing = jnp.maximum(t_idx - s_idx, 0).astype(jnp.float32)
    causal = t_idx >= s_idx
    row_i = lax.broadcasted_iota(jnp.int32, (TURN, HD), 0)
    row_f = row_i.astype(jnp.float32)
    for h in range(HEADS):
        grid[h] = jnp.where(causal, jnp.exp(-decay_ref[h] * spacing), 0.0)
        qdec[h] = jnp.exp(-decay_ref[h] * (row_f + 1.0))
    for copy in loads[4:]:
        copy.wait()
    to_scalars.wait()

    def local(j, _):
        length = len_ref[j]
        live = row_i < length
        remain = jnp.maximum(length.astype(jnp.float32) - 1.0 - row_f, 0.0)
        for h in range(HEADS):
            cols = slice(h * HD, (h + 1) * HD)
            qh, kh, vh = q[j, :, cols], k[j, :, cols], v[j, :, cols]
            scores = lax.dot_general(
                qh, kh, (((1,), (1,)), ((), ())), preferred_element_type=jnp.float32
            )
            weights = (scores * grid[h]).astype(jnp.bfloat16)
            att[j, :, cols] = jnp.dot(weights, vh, preferred_element_type=jnp.float32)
            kdec = jnp.where(
                live, kh.astype(jnp.float32) * jnp.exp(-decay_ref[h] * remain), 0.0
            ).astype(jnp.bfloat16)
            upd[j, h] = lax.dot_general(
                kdec, vh, (((0,), (0,)), ((), ())), preferred_element_type=jnp.float32
            )
        return 0

    lax.fori_loop(0, CONV, local, 0)

    for c in range(CHUNKS):
        wait_bytes(gath[c], a_sem.at[1, c])

        def pick(d, _):
            for jj in range(PER):
                outg[c, d, jj] = gath[c][src_ref[0, d * CONV + c * PER + jj], jj]
            return 0

        lax.fori_loop(0, nb, pick, 0, unroll=4)
        for t in peers:
            pltpu.make_async_remote_copy(
                src_ref=outg.at[c, t], dst_ref=carr.at[convs(c), piece(me), :],
                send_sem=b_sem.at[0, c], recv_sem=b_sem.at[1, c],
                device_id=(t, m), device_id_type=MESH,
            ).start()
        pltpu.make_async_copy(
            outg.at[c, me], carr.at[convs(c), piece(me), :], b_sem.at[1, c]
        ).start()

    def read_carried(j):
        wide[0] = carr[j].astype(jnp.float32)

    def head(h):
        return wide[0, pl.ds(h, HD, stride=HEADS), :]

    def finish(c):
        wait_bytes(carr.at[convs(c)], b_sem.at[1, c])
        for jj in range(PER):
            j = c * PER + jj
            live = row_i < len_ref[j]
            read_carried(j)
            square = jnp.zeros((TURN, HD), jnp.float32)
            for h in range(HEADS):
                cols = slice(h * HD, (h + 1) * HD)
                term = jnp.dot(
                    q[j, :, cols], head(h).astype(jnp.bfloat16), preferred_element_type=jnp.float32
                )
                a = jnp.where(live, att[j, :, cols] + term * qdec[h], 0.0)
                att[j, :, cols] = a
                square = square + a * a
            high = square.astype(jnp.bfloat16)
            low = (square - high.astype(jnp.float32)).astype(jnp.bfloat16)
            row = lax.dot_general(
                jnp.ones((8, 2 * HD), jnp.bfloat16), jnp.concatenate([high, low], axis=1),
                (((1,), (1,)), ((), ())), preferred_element_type=jnp.float32,
            )
            sums[c, m, pl.ds(jj, 1), :] = row[0:1]
        for d in range(1, nm):
            pltpu.make_async_remote_copy(
                src_ref=sums.at[c, m], dst_ref=sums.at[c, m], send_sem=m_sem.at[0, c],
                recv_sem=m_sem.at[1, c], device_id=(me, lax.rem(m + d, nm)), device_id_type=MESH,
            ).start()

    def update(c):
        for jj in range(PER):
            j = c * PER + jj
            length = len_ref[j].astype(jnp.float32)
            read_carried(j)
            for h in range(HEADS):
                keep = jnp.exp(jnp.full((HD, HD), -decay_ref[h] * length, jnp.float32))
                wide[1, pl.ds(h, HD, stride=HEADS), :] = keep * head(h) + upd[j, h]
            sout[j] = wide[1].astype(jnp.bfloat16)

    def normalize(c):
        wait_bytes(sums.at[c, pl.ds(0, nm - 1)], m_sem.at[1, c])
        for jj in range(PER):
            j = c * PER + jj
            total = lax.dot_general(
                sums[c, :, jj, :], jnp.ones((nm, HD), jnp.float32), (((0,), (0,)), ((), ())),
                preferred_element_type=jnp.float32, precision=HIGH,
            )
            scale = lax.rsqrt(total / (nm * WIDTH) + EPS)
            for h in range(HEADS):
                cols = slice(h * HD, (h + 1) * HD)
                out[j, :, cols] = (att[j, :, cols] * scale * gain_ref[:, cols]).astype(jnp.bfloat16)

    for c in range(CHUNKS):
        finish(c)
    for c in range(CHUNKS):
        update(c)
    for c in range(CHUNKS):
        normalize(c)

    for c in range(CHUNKS):
        wait_bytes(gath[c].at[pl.ds(0, nb - 1)], a_sem.at[0, c])
        wait_bytes(outg.at[c, pl.ds(0, nb - 1)], b_sem.at[0, c])
        wait_bytes(sums.at[c, pl.ds(0, nm - 1)], m_sem.at[0, c])


def store_kernel(out, sout, out_hbm, sout_hbm, sems):
    copies = [
        pltpu.make_async_copy(out, out_hbm, sems.at[0]),
        pltpu.make_async_copy(sout, sout_hbm, sems.at[1]),
    ]
    for copy in copies:
        copy.start()
    for copy in copies:
        copy.wait()


def per_device(nb, nm, queries, keys, values_in, state_in, decay_rate, norm_gain, turn_len, relocation):
    state = state_in.reshape(CONV, HEADS, HD, HD).transpose(0, 2, 1, 3).reshape(CONV, ROWS, HD)
    nx = min(NX, nb)
    nz = nb // nx
    rows = ROWS // nb
    places = relocation.shape[0]
    bf16, f32 = jnp.bfloat16, jnp.float32
    anywhere = pl.BlockSpec(memory_space=pl.ANY)
    in_vmem = pl.BlockSpec(memory_space=pltpu.VMEM)
    operands = [
        pltpu.with_memory_space_constraint(a, pltpu.HBM)
        for a in (
            decay_rate, turn_len, relocation.reshape(1, places), norm_gain.reshape(1, WIDTH),
            queries, keys, values_in, state,
        )
    ]
    layer_out, state_out = pl.pallas_call(
        functools.partial(kernel, nx, nz, nm),
        out_shape=(
            pltpu.VMEM((CONV, TURN, WIDTH), bf16),
            pltpu.VMEM((CONV, ROWS, HD), bf16),
        ),
        in_specs=[anywhere] * 8,
        out_specs=(in_vmem, in_vmem),
        scratch_shapes=[
            pltpu.SMEM((HEADS,), f32),
            pltpu.SMEM((CONV,), jnp.int32),
            pltpu.SMEM((1, places), jnp.int32),
            pltpu.VMEM((1, places), jnp.int32),
            pltpu.VMEM((1, places), jnp.int32),
            pltpu.VMEM((1, WIDTH), f32),
            pltpu.VMEM((CONV, TURN, WIDTH), bf16),
            pltpu.VMEM((CONV, TURN, WIDTH), bf16),
            pltpu.VMEM((CONV, TURN, WIDTH), bf16),
            pltpu.VMEM((CONV, TURN, WIDTH), f32),
            pltpu.VMEM((CONV, HEADS, HD, HD), f32),
            pltpu.VMEM((HEADS, TURN, TURN), f32),
            pltpu.VMEM((HEADS, TURN, HD), f32),
            pltpu.VMEM((CHUNKS, nb, PER, rows, HD), bf16),
            pltpu.VMEM((CONV, ROWS, HD), bf16),
            pltpu.VMEM((2, ROWS, HD), f32),
            pltpu.VMEM((CHUNKS, nm, PER, TURN), f32),
            pltpu.SemaphoreType.DMA((5,)),
            pltpu.SemaphoreType.DMA((3,)),
        ]
        + [pltpu.SemaphoreType.DMA((2, CHUNKS))] * 3
        + [pltpu.VMEM((nb, PER, rows, HD), bf16)] * CHUNKS,
        compiler_params=pltpu.CompilerParams(
            collective_id=0, has_side_effects=True, vmem_limit_bytes=40 << 20
        ),
    )(*operands)
    layer_out, state_out = pl.pallas_call(
        store_kernel,
        out_shape=(
            jax.ShapeDtypeStruct((CONV, TURN, WIDTH), bf16),
            jax.ShapeDtypeStruct((CONV, ROWS, HD), bf16),
        ),
        in_specs=[anywhere] * 2,
        out_specs=(anywhere, anywhere),
        scratch_shapes=[pltpu.SemaphoreType.DMA((2,))],
    )(*(pltpu.with_memory_space_constraint(a, pltpu.VMEM) for a in (layer_out, state_out)))
    state_out = state_out.reshape(CONV, HD, HEADS, HD).transpose(0, 2, 1, 3)
    return layer_out, state_out.reshape(CONV, HEADS, HD * HD)


def solution(mesh):
    nb, nm = mesh.shape["rollout"], mesh.shape["mp"]
    in_specs = (
        P("rollout", None, "mp"),
        P("rollout", None, "mp"),
        P("rollout", None, "mp"),
        P("rollout", "mp", None),
        P("mp"),
        P("mp"),
        P("rollout"),
        P(),
    )
    out_specs = (P("rollout", None, "mp"), P("rollout", "mp", None))
    return jax.shard_map(
        functools.partial(per_device, nb, nm),
        mesh=mesh, in_specs=in_specs, out_specs=out_specs, check_vma=False,
    )
```

```python
import functools

import jax
import jax.numpy as jnp
from jax import lax
from jax.experimental import pallas as pl
from jax.experimental.pallas import tpu as pltpu
from jax.sharding import PartitionSpec as P

EPS = 1e-05
MESH = pl.DeviceIdType.MESH
HD = 128
TURN = 256
CONV = 4
HEADS = 4
WIDTH = HEADS * HD
ROWS = HEADS * HD
SIZES = (2, 2)
STARTS = (0, 2)
CHUNKS = len(SIZES)
ZORDER = (4, 3, 5, 2, 6, 1, 7)
ORDER = [(dz, dx) for dz in (4, 3, 5, 2, 6, 1, 7, 0) for dx in (2, 1, 3, 0) if dz or dx]
NX = 4
HIGH = lax.Precision.HIGHEST


def wait_bytes(ref, sem):
    pltpu.make_async_copy(ref, ref, sem).wait()


def kernel(
    nx, nz, nm,
    decay_hbm, len_hbm, reloc_hbm, gain_hbm, q_hbm, k_hbm, v_hbm, state_hbm,
    out, sout,
    decay_ref, len_ref, src_ref, src_row, reloc_ref, gain_ref,
    q, k, v, att, upd, grid, qdec, carr, wide,
    small_sem, load_sem, a_sem, b_sem, m_sem, row_sem, *slots,
):
    gath, outg, sums = slots[:CHUNKS], slots[CHUNKS:2 * CHUNKS], slots[2 * CHUNKS:]
    nb = nz * nx
    me = lax.axis_index("rollout")
    m = lax.axis_index("mp")
    z = me // nx
    x = lax.rem(me, nx)
    rows = ROWS // nb

    def peer(dz, dx):
        return lax.rem(z + dz, nz) * nx + lax.rem(x + dx, nx)

    column = [peer(dz, 0) for dz in ZORDER if dz < nz]
    row = [peer(0, dx) for dx in (2, 1, 3) if dx < nx]
    rest = [peer(dz, dx) for dz, dx in ORDER if 0 < dz < nz and 0 < dx < nx]
    peers = column + row + rest
    barrier = pltpu.get_barrier_semaphore()
    for t in column + row:
        pl.semaphore_signal(barrier, inc=1, device_id=(t, m), device_id_type=MESH)
    for d in range(1, nm):
        pl.semaphore_signal(barrier, inc=1, device_id=(me, lax.rem(m + d, nm)), device_id_type=MESH)

    def piece(t):
        return pl.ds(pl.multiple_of(t * rows, rows), rows)

    def convs(c):
        return pl.ds(STARTS[c], SIZES[c])

    loads = [
        pltpu.make_async_copy(source, target, small_sem.at[n])
        for n, (source, target) in enumerate((
            (reloc_hbm, reloc_ref), (decay_hbm, decay_ref), (len_hbm, len_ref), (gain_hbm, gain_ref),
        ))
    ] + [
        pltpu.make_async_copy(source, target, load_sem.at[n])
        for n, (source, target) in enumerate(((k_hbm, k), (v_hbm, v), (q_hbm, q)))
    ]
    pl.semaphore_wait(barrier, nz - 1 + nx - 1 + nm - 1)
    for t in row:
        pl.semaphore_signal(row_sem, inc=1, device_id=(t, m), device_id_type=MESH)

    for c in range(CHUNKS):
        for t in peers:
            if c == 0 and t is rest[0]:
                pl.semaphore_wait(row_sem, nx - 1)
            pltpu.make_async_remote_copy(
                src_ref=state_hbm.at[convs(c), piece(t), :], dst_ref=gath[c].at[me],
                send_sem=a_sem.at[0, c], recv_sem=a_sem.at[1, c],
                device_id=(t, m), device_id_type=MESH,
            ).start()
        pltpu.make_async_copy(
            state_hbm.at[convs(c), piece(me), :], gath[c].at[me], a_sem.at[1, c]
        ).start()
        if c == 0:
            for copy in loads:
                copy.start()

    for copy in loads[:4]:
        copy.wait()
    places = src_row.shape[1]
    came = jnp.broadcast_to(reloc_ref[...], (places, places)).T
    old = lax.broadcasted_iota(jnp.int32, (places, places), 0) // CONV
    place = lax.broadcasted_iota(jnp.int32, (places, places), 1)
    src_row[...] = jnp.max(jnp.where(came == place, old, 0), axis=0, keepdims=True)
    to_scalars = pltpu.make_async_copy(src_row, src_ref, small_sem.at[4])
    to_scalars.start()

    t_idx = lax.broadcasted_iota(jnp.int32, (TURN, TURN), 0)
    s_idx = lax.broadcasted_iota(jnp.int32, (TURN, TURN), 1)
    spacing = jnp.maximum(t_idx - s_idx, 0).astype(jnp.float32)
    causal = t_idx >= s_idx
    row_i = lax.broadcasted_iota(jnp.int32, (TURN, HD), 0)
    row_f = row_i.astype(jnp.float32)
    for h in range(HEADS):
        grid[h] = jnp.where(causal, jnp.exp(-decay_ref[h] * spacing), 0.0)
        qdec[h] = jnp.exp(-decay_ref[h] * (row_f + 1.0))
    for copy in loads[4:]:
        copy.wait()
    to_scalars.wait()

    def local(j, _):
        length = len_ref[j]
        live = row_i < length
        remain = jnp.maximum(length.astype(jnp.float32) - 1.0 - row_f, 0.0)
        for h in range(HEADS):
            cols = slice(h * HD, (h + 1) * HD)
            qh, kh, vh = q[j, :, cols], k[j, :, cols], v[j, :, cols]
            scores = lax.dot_general(
                qh, kh, (((1,), (1,)), ((), ())), preferred_element_type=jnp.float32
            )
            weights = (scores * grid[h]).astype(jnp.bfloat16)
            att[j, :, cols] = jnp.dot(weights, vh, preferred_element_type=jnp.float32)
            kdec = jnp.where(
                live, kh.astype(jnp.float32) * jnp.exp(-decay_ref[h] * remain), 0.0
            ).astype(jnp.bfloat16)
            upd[j, h] = lax.dot_general(
                kdec, vh, (((0,), (0,)), ((), ())), preferred_element_type=jnp.float32
            )
        return 0

    lax.fori_loop(0, CONV, local, 0)

    for c in range(CHUNKS):
        wait_bytes(gath[c], a_sem.at[1, c])

        def pick(t):
            for jj in range(SIZES[c]):
                outg[c][t, jj] = gath[c][src_ref[0, t * CONV + STARTS[c] + jj], jj]

        for t in peers:
            pick(t)
            pltpu.make_async_remote_copy(
                src_ref=outg[c].at[t], dst_ref=carr.at[convs(c), piece(me), :],
                send_sem=b_sem.at[0, c], recv_sem=b_sem.at[1, c],
                device_id=(t, m), device_id_type=MESH,
            ).start()
        pick(me)
        pltpu.make_async_copy(
            outg[c].at[me], carr.at[convs(c), piece(me), :], b_sem.at[1, c]
        ).start()

    def read_carried(j):
        wide[0] = carr[j].astype(jnp.float32)

    def head(h):
        return wide[0, pl.ds(h, HD, stride=HEADS), :]

    def finish(c):
        wait_bytes(carr.at[convs(c)], b_sem.at[1, c])
        for jj in range(SIZES[c]):
            j = STARTS[c] + jj
            live = row_i < len_ref[j]
            read_carried(j)
            square = jnp.zeros((TURN, HD), jnp.float32)
            for h in range(HEADS):
                cols = slice(h * HD, (h + 1) * HD)
                term = jnp.dot(
                    q[j, :, cols], head(h).astype(jnp.bfloat16), preferred_element_type=jnp.float32
                )
                a = jnp.where(live, att[j, :, cols] + term * qdec[h], 0.0)
                att[j, :, cols] = a
                square = square + a * a
            high = square.astype(jnp.bfloat16)
            low = (square - high.astype(jnp.float32)).astype(jnp.bfloat16)
            row = lax.dot_general(
                jnp.ones((8, 2 * HD), jnp.bfloat16), jnp.concatenate([high, low], axis=1),
                (((1,), (1,)), ((), ())), preferred_element_type=jnp.float32,
            )
            sums[c][m, pl.ds(jj, 1), :] = row[0:1]
        for d in sorted(range(1, nm), key=lambda d: -min(d, nm - d)):
            pltpu.make_async_remote_copy(
                src_ref=sums[c].at[m], dst_ref=sums[c].at[m], send_sem=m_sem.at[0, c],
                recv_sem=m_sem.at[1, c], device_id=(me, lax.rem(m + d, nm)), device_id_type=MESH,
            ).start()

    def update(c):
        for jj in range(SIZES[c]):
            j = STARTS[c] + jj
            length = len_ref[j].astype(jnp.float32)
            read_carried(j)
            for h in range(HEADS):
                keep = jnp.exp(jnp.full((HD, HD), -decay_ref[h] * length, jnp.float32))
                wide[1, pl.ds(h, HD, stride=HEADS), :] = keep * head(h) + upd[j, h]
            sout[j] = wide[1].astype(jnp.bfloat16)

    def normalize(c):
        wait_bytes(sums[c].at[pl.ds(0, nm - 1)], m_sem.at[1, c])
        for jj in range(SIZES[c]):
            j = STARTS[c] + jj
            total = lax.dot_general(
                sums[c][:, jj, :], jnp.ones((nm, HD), jnp.float32), (((0,), (0,)), ((), ())),
                preferred_element_type=jnp.float32, precision=HIGH,
            )
            scale = lax.rsqrt(total / (nm * WIDTH) + EPS)
            for h in range(HEADS):
                cols = slice(h * HD, (h + 1) * HD)
                out[j, :, cols] = (att[j, :, cols] * scale * gain_ref[:, cols]).astype(jnp.bfloat16)

    for c in range(CHUNKS):
        finish(c)
    for c in range(CHUNKS):
        update(c)
    for c in range(CHUNKS):
        normalize(c)

    for c in range(CHUNKS):
        wait_bytes(gath[c].at[pl.ds(0, nb - 1)], a_sem.at[0, c])
        wait_bytes(outg[c].at[pl.ds(0, nb - 1)], b_sem.at[0, c])
        wait_bytes(sums[c].at[pl.ds(0, nm - 1)], m_sem.at[0, c])


def store_kernel(out, sout, out_hbm, sout_hbm, sems):
    copies = [
        pltpu.make_async_copy(out, out_hbm, sems.at[0]),
        pltpu.make_async_copy(sout, sout_hbm, sems.at[1]),
    ]
    for copy in copies:
        copy.start()
    for copy in copies:
        copy.wait()


def per_device(nb, nm, queries, keys, values_in, state_in, decay_rate, norm_gain, turn_len, relocation):
    state = state_in.reshape(CONV, HEADS, HD, HD).transpose(0, 2, 1, 3).reshape(CONV, ROWS, HD)
    nx = min(NX, nb)
    nz = nb // nx
    rows = ROWS // nb
    places = relocation.shape[0]
    bf16, f32 = jnp.bfloat16, jnp.float32
    anywhere = pl.BlockSpec(memory_space=pl.ANY)
    in_vmem = pl.BlockSpec(memory_space=pltpu.VMEM)
    operands = [
        pltpu.with_memory_space_constraint(a, pltpu.HBM)
        for a in (
            decay_rate, turn_len, relocation.reshape(1, places), norm_gain.reshape(1, WIDTH),
            queries, keys, values_in, state,
        )
    ]
    layer_out, state_out = pl.pallas_call(
        functools.partial(kernel, nx, nz, nm),
        out_shape=(
            pltpu.VMEM((CONV, TURN, WIDTH), bf16),
            pltpu.VMEM((CONV, ROWS, HD), bf16),
        ),
        in_specs=[anywhere] * 8,
        out_specs=(in_vmem, in_vmem),
        scratch_shapes=[
            pltpu.SMEM((HEADS,), f32),
            pltpu.SMEM((CONV,), jnp.int32),
            pltpu.SMEM((1, places), jnp.int32),
            pltpu.VMEM((1, places), jnp.int32),
            pltpu.VMEM((1, places), jnp.int32),
            pltpu.VMEM((1, WIDTH), f32),
            pltpu.VMEM((CONV, TURN, WIDTH), bf16),
            pltpu.VMEM((CONV, TURN, WIDTH), bf16),
            pltpu.VMEM((CONV, TURN, WIDTH), bf16),
            pltpu.VMEM((CONV, TURN, WIDTH), f32),
            pltpu.VMEM((CONV, HEADS, HD, HD), f32),
            pltpu.VMEM((HEADS, TURN, TURN), f32),
            pltpu.VMEM((HEADS, TURN, HD), f32),
            pltpu.VMEM((CONV, ROWS, HD), bf16),
            pltpu.VMEM((2, ROWS, HD), f32),
            pltpu.SemaphoreType.DMA((5,)),
            pltpu.SemaphoreType.DMA((3,)),
        ]
        + [pltpu.SemaphoreType.DMA((2, CHUNKS))] * 3
        + [pltpu.SemaphoreType.REGULAR]
        + [pltpu.VMEM((nb, n, rows, HD), bf16) for n in SIZES * 2]
        + [pltpu.VMEM((nm, n, TURN), f32) for n in SIZES],
        compiler_params=pltpu.CompilerParams(
            collective_id=0, has_side_effects=True, vmem_limit_bytes=40 << 20
        ),
    )(*operands)
    layer_out, state_out = pl.pallas_call(
        store_kernel,
        out_shape=(
            jax.ShapeDtypeStruct((CONV, TURN, WIDTH), bf16),
            jax.ShapeDtypeStruct((CONV, ROWS, HD), bf16),
        ),
        in_specs=[anywhere] * 2,
        out_specs=(anywhere, anywhere),
        scratch_shapes=[pltpu.SemaphoreType.DMA((2,))],
    )(*(pltpu.with_memory_space_constraint(a, pltpu.VMEM) for a in (layer_out, state_out)))
    state_out = state_out.reshape(CONV, HD, HEADS, HD).transpose(0, 2, 1, 3)
    return layer_out, state_out.reshape(CONV, HEADS, HD * HD)


def solution(mesh):
    nb, nm = mesh.shape["rollout"], mesh.shape["mp"]
    in_specs = (
        P("rollout", None, "mp"),
        P("rollout", None, "mp"),
        P("rollout", None, "mp"),
        P("rollout", "mp", None),
        P("mp"),
        P("mp"),
        P("rollout"),
        P(),
    )
    out_specs = (P("rollout", None, "mp"), P("rollout", "mp", None))
    return jax.shard_map(
        functools.partial(per_device, nb, nm),
        mesh=mesh, in_specs=in_specs, out_specs=out_specs, check_vma=False,
    )
```
